32 devices in a mesh: seg: 4 (over z), sec: 8 (over y, x, core).
Axes of the slice: x: 2, y: 2, z: 4, core: 2. Of those that a mesh axis runs over, the one named last changes fastest.
Arguments:
- boundary_env: bfloat16 [4, 8, 13, 256, 256], P('seg', 'sec'), may hold values from -6 to 6
- site_block_tensors: bfloat16 [8, 8, 4, 256, 256], P('seg', 'sec'), may hold values from -0.375 to 0.375
- mpo_tensors: bfloat16 [8, 4, 13, 13], P('seg'), may hold values from -1.75 to 1.75
- block_mask: int32 [8, 8, 4], P('seg', 'sec'), may hold values 0 or 1
- sector_dims: int32 [8], replicated, may hold values from 128 to 256, as said below
Outputs:
- handed_env: bfloat16 [4, 8, 13, 256, 256], P('seg', 'sec')
The draws below stay inside these ranges and needn't reach their ends.
Inputs may be any that keep to these rules, and one draw needn't show every extreme that they name: `sector_dims`: each entry is 128 or 256, and both occur in every draw.
All inputs are finite; a program needn't handle non-finite values. No bound on the sum of `block_mask` on one device may be relied on, other than what follows from the above.
Results may differ from the reference program's by a relative error of at most 0.02.
Values may be sent and summed in bfloat16 or wider, within the bound.
No kernel may reach another device: no remote copies, remote signals or barrier semaphores. Data moves between devices by JAX's collectives and lax.ppermute only.
A program may use at most 64 MiB of HBM per device.

```python
import jax
import jax.numpy as jnp
from jax import lax

WB = 13
CAP = 256
ND = 4
SITES = 2
NSEG = 4
NSEC = 8
CHAIN_SITES = 8


def draw_sector_dims(key, part):
    keys = jax.random.split(key, 3)
    coin_flips = jax.random.randint(keys[0], (NSEC,), 0, 2)
    big_slot = jax.random.randint(keys[1], (), 0, NSEC)
    small_slot = (big_slot + 1 + jax.random.randint(keys[2], (), 0, NSEC - 1)) % NSEC
    coin_flips = coin_flips.at[big_slot].set(1).at[small_slot].set(0)
    return (CAP // 2 * (1 + coin_flips)).astype(jnp.int32)


def plant(drawn, key, low, largest):
    index_at = [jax.random.randint(jax.random.fold_in(key, axis), (), 0, length) for axis, length in enumerate(drawn.shape)]
    main_axis = drawn.shape.index(max(drawn.shape))
    next_to = index_at[:main_axis] + [(index_at[main_axis] + 1) % drawn.shape[main_axis]] + index_at[main_axis + 1:]
    return drawn.at[tuple(index_at)].set(low).at[tuple(next_to)].set(largest)


def level_of(key, shape, cuts, smallest, high):
    def one(position, shards_of):
        draws = jax.random.uniform(jax.random.fold_in(jax.random.fold_in(key, 6), position), (shards_of,), jnp.float32, smallest / len(cuts), high / len(cuts))
        return jnp.repeat(jnp.exp(draws), shape[position] // shards_of).reshape((-1,) + (1,) * (len(shape) - position - 1))

    factor_of = one(*cuts[0])
    for cut in cuts[1:]:
        factor_of = factor_of * one(*cut)
    return factor_of


def scatter_about(stream_key, dims, scale, limit, pieces=(), dtype=jnp.bfloat16):
    values = scale * jax.random.normal(stream_key, dims, jnp.float32)
    if pieces:
        values = values * level_of(stream_key, dims, pieces, -0.22, 0.18)
    return jnp.clip(values, -limit, limit).astype(dtype)


def setup_inputs(seed: int = 0) -> dict:
    key_list = jax.random.split(jax.random.key(seed), 6)
    return {
        "boundary_env": scatter_about(key_list[0], (NSEG, NSEC, WB, CAP, CAP), 1.0, 6.0, ((0, 4), (1, 8))),
        "site_block_tensors": scatter_about(key_list[1], (CHAIN_SITES, NSEC, 4, CAP, CAP), CAP ** -0.5, 0.375, ((0, 4), (1, 8))),
        "mpo_tensors": scatter_about(key_list[2], (CHAIN_SITES, 4, WB, WB), WB ** -0.5, 1.75, ((0, 4),)),
        "block_mask": plant((jax.random.randint(key_list[3], (CHAIN_SITES, NSEC, 4), 0, 4) < 3).astype(jnp.int32), jax.random.fold_in(key_list[3], 1), 0, 1),
        "sector_dims": draw_sector_dims(jax.random.fold_in(key_list[5], 71), 0),
    }


def sector_tables(sector_dims):
    sectors = jnp.arange(NSEC)
    offsets = jnp.array([0, ND, 1, ND + 1])
    down_step = jnp.array([0, 0, 1, 1])
    targets = sectors[:, None] + offsets[None, :]
    allowed = (targets < NSEC) & ((down_step[None, :] == 0) | ((sectors % ND)[:, None] < ND - 1))
    target_dims = jnp.where(allowed, sector_dims[jnp.clip(targets, 0, NSEC - 1)], 0)
    line = jnp.arange(CAP)
    row_live = line[None, :] < sector_dims[:, None]
    col_live = line[None, None, :] < target_dims[:, :, None]
    return allowed, row_live, col_live


def sector_update(left_environ_tensor, block_list, weight_factors):
    output_collection = []
    for carry_state in range(4):
        merged_mixture = jnp.einsum('umi,ue->emi', left_environ_tensor.astype(jnp.float32), weight_factors[carry_state].astype(jnp.float32)).astype(jnp.bfloat16)
        combined_mixture = jnp.einsum('gip,pq->giq', merged_mixture.astype(jnp.float32), block_list[carry_state].astype(jnp.float32)).astype(jnp.bfloat16)
        output_collection.append(jnp.einsum('ba,vbc->vac', block_list[carry_state].astype(jnp.float32), combined_mixture.astype(jnp.float32)).astype(jnp.bfloat16))
    return jnp.stack(output_collection)


def move_up(values, steps):
    filler = jnp.zeros((steps,) + values.shape[1:], jnp.float32)
    return jnp.concatenate([filler, values[:-steps].astype(jnp.float32)], axis=0)


def reference(boundary_env, site_block_tensors, mpo_tensors, block_mask, sector_dims):
    allowed, row_live, col_live = sector_tables(sector_dims)
    env_live = (row_live[:, None, :, None] & row_live[:, None, None, :]).astype(jnp.bfloat16)

    def one_segment(segment):
        left_environ_tensor = boundary_env[segment] * env_live
        for site_pos in range(SITES):
            chain_pos = segment * SITES + site_pos
            present = block_mask[chain_pos] * allowed.astype(jnp.int32)
            factor = present[:, :, None, None] * row_live[:, None, :, None].astype(jnp.int32) * col_live[:, :, None, :].astype(jnp.int32)
            block_list = site_block_tensors[chain_pos] * factor.astype(jnp.bfloat16)
            weight_factors = mpo_tensors[chain_pos]
            partial_value = lax.map(lambda pair: sector_update(pair[0], pair[1], weight_factors), (left_environ_tensor, block_list))
            total = partial_value[:, 0].astype(jnp.float32) + move_up(partial_value[:, 1], ND)
            total = total + move_up(partial_value[:, 2], 1) + move_up(partial_value[:, 3], ND + 1)
            left_environ_tensor = total.astype(jnp.bfloat16)
        return left_environ_tensor

    finals = lax.map(one_segment, jnp.arange(NSEG).astype(jnp.int32))
    return jnp.concatenate([jnp.zeros_like(finals[:1]), finals[:-1]], axis=0)
```

```python
import jax
import jax.numpy as jnp
from jax import lax
from jax.experimental import pallas as pl
from jax.experimental.pallas import tpu as pltpu
from jax.sharding import PartitionSpec as P

ND = 4
ROWS = 16
VMEM_BYTES = 56 * 2**20


def from_behind(shard, axis, by):
    count = lax.axis_size(axis)
    pairs = [(i, i + by) for i in range(count) if 0 <= i + by < count]
    return lax.ppermute(shard, axis, pairs)


def shift_column(shard):
    count = lax.axis_size("sec")
    return lax.ppermute(shard, "sec", [(q, q + 1) for q in range(count - 1) if q % ND < ND - 1])


def widen(weights):
    eye = jnp.eye(ROWS, dtype=weights.dtype)
    return weights.transpose(0, 2, 1)[:, :, None, :, None] * eye[None, None, :, None, :]


def product_kernel(plan, out_sizes, sources, *refs):
    env_refs = refs[:sources]
    mix_refs = refs[sources:2 * sources]
    block_ref = refs[2 * sources]
    out_refs = refs[2 * sources + 1:2 * sources + 1 + len(out_sizes)]
    scratch = refs[2 * sources + 1 + len(out_sizes):]
    mixed_refs, flipped_ref = scratch[:-1], scratch[-1]
    channels, cap, _ = env_refs[0].shape
    for k in range(block_ref.shape[0]):
        flipped_ref[k] = block_ref[k].T
    for env_ref, mix_ref, mixed_ref in zip(env_refs, mix_refs, mixed_refs):
        count = mixed_ref.shape[0]

        def mix(g, _):
            rows = pl.ds(pl.multiple_of(g * ROWS, ROWS), ROWS)
            piece = env_ref[:, rows, :].reshape(channels * ROWS, cap)
            mixed = jnp.dot(mix_ref[...], piece, preferred_element_type=jnp.float32)
            mixed_ref[:, rows, :] = mixed.astype(jnp.bfloat16).reshape(count, ROWS, cap)
            return 0

        lax.fori_loop(0, cap // ROWS, mix, 0, unroll=2)
    width = out_refs[0].shape[1]

    def channel(v, _):
        totals = {}
        for source, states in enumerate(plan):
            for place, (block, out, slot) in enumerate(states):
                blended = jnp.dot(
                    mixed_refs[source][place * width + v], block_ref[block], preferred_element_type=jnp.float32
                ).astype(jnp.bfloat16)
                part = jnp.dot(flipped_ref[block], blended, preferred_element_type=jnp.float32)
                key = (out, slot)
                totals[key] = part if key not in totals else totals[key] + part
        for (out, slot), total in totals.items():
            out_refs[out][slot, v] = total.astype(jnp.bfloat16)
        return 0

    lax.fori_loop(0, width, channel, 0)


def products(plan, out_sizes, envs, mixers, blocks, width):
    cap = envs[0].shape[-1]
    work = sum(len(states) for states in plan)
    kernel = lambda *refs: product_kernel(plan, out_sizes, len(envs), *refs)
    return pl.pallas_call(
        kernel,
        out_shape=[jax.ShapeDtypeStruct((n, width, cap, cap), jnp.bfloat16) for n in out_sizes],
        in_specs=[pl.BlockSpec(memory_space=pltpu.VMEM)] * (2 * len(envs) + 1),
        out_specs=[pl.BlockSpec(memory_space=pltpu.VMEM)] * len(out_sizes),
        scratch_shapes=[pltpu.VMEM((len(states) * width, cap, cap), jnp.bfloat16) for states in plan]
        + [pltpu.VMEM(blocks.shape, jnp.bfloat16)],
        compiler_params=pltpu.CompilerParams(vmem_limit_bytes=VMEM_BYTES),
        cost_estimate=pl.CostEstimate(
            flops=6 * work * width * cap**3, bytes_accessed=4 * 2**20, transcendentals=0
        ),
    )(*envs, *mixers, blocks)


def masked_blocks(site_block_tensors, block_mask, sector_dims):
    capacity = site_block_tensors.shape[-1]
    sector_total = lax.axis_size("sec")
    sector_id = lax.axis_index("sec")
    offsets = jnp.array([0, ND, 1, ND + 1])
    down_step = jnp.array([0, 0, 1, 1])
    targets = sector_id + offsets
    allowed = (targets < sector_total) & ((down_step == 0) | (sector_id % ND < ND - 1))
    sectors = jnp.arange(sector_total)
    own_dims = jnp.sum(jnp.where(sectors == sector_id, sector_dims, 0))
    target_dims = jnp.sum(
        jnp.where(sectors[None, :] == targets[:, None], sector_dims[None, :], 0), axis=1
    )
    target_dims = jnp.where(allowed, target_dims, 0)
    line = jnp.arange(capacity)
    row_live = line < own_dims
    col_live = line[None, :] < target_dims[:, None]
    present = (block_mask[:, 0] * allowed.astype(jnp.int32)).astype(jnp.bfloat16)
    live = row_live[None, :, None] & col_live[:, None, :]
    return jnp.where(live[None], site_block_tensors[:, 0] * present[:, :, None, None], 0)


def two_rows(boundary_env, site_block_tensors, mpo_tensors, block_mask, sector_dims):
    env = boundary_env[0, 0]
    channels = env.shape[0]
    near_env = shift_column(env)
    blocks = masked_blocks(site_block_tensors, block_mask, sector_dims)
    near_blocks = shift_column(blocks[0, 2:4])
    below = lax.ppermute(blocks[1, 0::2], "sec", [(ND + j, j) for j in range(ND)])
    wide = [widen(mpo_tensors[n]) for n in range(2)]
    span = channels * ROWS

    def mixer(n, states, low, high):
        return jnp.concatenate([wide[n][s, low:high] for s in states]).reshape(-1, span)

    (middle,) = products(
        (((0, 0, 0), (1, 0, 1)), ((2, 0, 0), (3, 0, 1))), (2,),
        (env, near_env), (mixer(0, (0, 1), 0, channels), mixer(0, (2, 3), 0, channels)),
        jnp.concatenate([blocks[0, 0:2], near_blocks]), channels,
    )
    last_blocks = jnp.concatenate([blocks[1], below])
    handed = []
    cuts = [0, 4, 7, 10, channels]
    for low, high in zip(cuts[:-1], cuts[1:]):
        stay, up = products(
            (((0, 0, 0), (1, 0, 1), (2, 1, 0), (3, 1, 1)), ((4, 0, 1), (5, 1, 1))), (2, 2),
            (middle[0], middle[1]), (mixer(1, (0, 1, 2, 3), low, high), mixer(1, (0, 2), low, high)),
            last_blocks, high - low,
        )
        arrived = shift_column(up)
        both = stay.astype(jnp.float32) + arrived.astype(jnp.float32)
        from_up = from_behind(both[1].astype(jnp.bfloat16), "sec", ND)
        total = (both[0] + from_up.astype(jnp.float32)).astype(jnp.bfloat16)
        handed.append(from_behind(total, "seg", 1))
    return jnp.concatenate(handed)[None, None]


def contract(left_environ_tensor, block_list, weight_factors):
    merged_mixture = jnp.einsum(
        "umi,ue->emi", left_environ_tensor, weight_factors, preferred_element_type=jnp.float32
    ).astype(jnp.bfloat16)
    combined_mixture = jnp.einsum(
        "gip,pq->giq", merged_mixture, block_list, preferred_element_type=jnp.float32
    ).astype(jnp.bfloat16)
    return jnp.einsum(
        "ba,vbc->vac", block_list, combined_mixture, preferred_element_type=jnp.float32
    ).astype(jnp.bfloat16)


def any_rows(boundary_env, site_block_tensors, mpo_tensors, block_mask, sector_dims):
    blocks = masked_blocks(site_block_tensors, block_mask, sector_dims)
    env = boundary_env[0, 0]
    for n in range(blocks.shape[0]):
        parts = [contract(env, blocks[n, s], mpo_tensors[n, s]) for s in range(4)]
        total = parts[0].astype(jnp.float32) + from_behind(parts[1], "sec", ND).astype(jnp.float32)
        total = total + from_behind(parts[2], "sec", 1).astype(jnp.float32)
        total = total + from_behind(parts[3], "sec", ND + 1).astype(jnp.float32)
        env = total.astype(jnp.bfloat16)
    return from_behind(env, "seg", 1)[None, None]


def solution(mesh):
    in_specs = (
        P("seg", "sec", None, None, None),
        P("seg", "sec", None, None, None),
        P("seg", None, None, None),
        P("seg", "sec", None),
        P(),
    )
    out_specs = P("seg", "sec", None, None, None)
    body = two_rows if mesh.shape["sec"] == 2 * ND else any_rows
    return jax.shard_map(body, mesh=mesh, in_specs=in_specs, out_specs=out_specs, check_vma=False)
```

```python
import jax
import jax.numpy as jnp
from jax import lax
from jax.experimental import pallas as pl
from jax.experimental.pallas import tpu as pltpu
from jax.sharding import PartitionSpec as P

ND = 4
ROWS = 16
PARTS = 2
UNROLL = True
VMEM_BYTES = 56 * 2**20


def from_behind(shard, axis, by):
    count = lax.axis_size(axis)
    pairs = [(i, i + by) for i in range(count) if 0 <= i + by < count]
    return lax.ppermute(shard, axis, pairs)


def shift_column(shard):
    count = lax.axis_size("sec")
    return lax.ppermute(shard, "sec", [(q, q + 1) for q in range(count - 1) if q % ND < ND - 1])


def mask_kernel(site_ref, mask_ref, dims_ref, *out_refs):
    cap = site_ref.shape[-1]
    total = dims_ref.shape[0]
    q = lax.axis_index("sec")
    rows = lax.broadcasted_iota(jnp.int32, (cap, cap), 0)
    columns = lax.broadcasted_iota(jnp.int32, (cap, cap), 1)
    own = rows < dims_ref[q]
    for out_ref, (site, states) in zip(out_refs, TAKEN):
        for place, s in enumerate(states):
            target = q + (0, ND, 1, ND + 1)[s]
            allowed = (mask_ref[site, 0, s] > 0) & (target < total)
            if s >= 2:
                allowed = allowed & (q % ND < ND - 1)
            width = jnp.where(allowed, dims_ref[jnp.minimum(target, total - 1)], 0)
            out_ref[place] = jnp.where(own & (columns < width), site_ref[site, 0, s], 0).astype(jnp.bfloat16)


TAKEN = ((0, (2, 3)), (1, (0, 2)), (0, (0, 1)), (1, (0, 1, 2, 3)))


def mask_blocks(site_block_tensors, block_mask, sector_dims):
    cap = site_block_tensors.shape[-1]
    return pl.pallas_call(
        mask_kernel,
        out_shape=[jax.ShapeDtypeStruct((len(states), cap, cap), jnp.bfloat16) for _, states in TAKEN],
        in_specs=[
            pl.BlockSpec(memory_space=pltpu.VMEM),
            pl.BlockSpec(memory_space=pltpu.SMEM),
            pl.BlockSpec(memory_space=pltpu.SMEM),
        ],
        out_specs=[pl.BlockSpec(memory_space=pltpu.VMEM)] * len(TAKEN),
        compiler_params=pltpu.CompilerParams(vmem_limit_bytes=VMEM_BYTES),
        cost_estimate=pl.CostEstimate(flops=10**6, bytes_accessed=2 * 2**20, transcendentals=0),
    )(site_block_tensors, block_mask, sector_dims)


def build_mixers(mpo_ref, site, plan, mixer_refs):
    channels = mpo_ref.shape[-1]
    span = channels * ROWS
    spread = (
        lax.broadcasted_iota(jnp.int32, (span, channels), 0) // ROWS
        == lax.broadcasted_iota(jnp.int32, (span, channels), 1)
    ).astype(jnp.bfloat16)
    same_row = (
        lax.broadcasted_iota(jnp.int32, (span, span), 0) % ROWS
        == lax.broadcasted_iota(jnp.int32, (span, span), 1) % ROWS
    )
    contract_last = (((1,), (1,)), ((), ()))
    for states, mixer_ref in zip(plan, mixer_refs):
        for place, (state, _, _) in enumerate(states):
            tall = lax.dot_general(spread, mpo_ref[site, state], contract_last, preferred_element_type=jnp.float32)
            wide = lax.dot_general(
                tall.astype(jnp.bfloat16), spread, contract_last, preferred_element_type=jnp.float32
            )
            mixer_ref[place * span:(place + 1) * span, :] = jnp.where(same_row, wide, 0.0).astype(jnp.bfloat16)


def product_kernel(site, plan, cuts, based, block_counts, *refs):
    sources = len(plan)
    outputs = 1 + max(out for states in plan for _, _, out in states)
    parts = len(cuts) - 1
    refs = list(refs)
    env_refs = [refs.pop(0) for _ in plan]
    base_refs = [refs.pop(0) for _ in range(outputs if based else 0)]
    mpo_ref = refs.pop(0)
    block_refs = [refs.pop(0) for _ in block_counts]
    out_refs = [[refs.pop(0) for _ in range(parts)] for _ in range(outputs)]
    mixed_refs = [refs.pop(0) for _ in plan]
    mixer_refs = [refs.pop(0) for _ in plan]
    flipped_ref = refs.pop(0)
    blocks = [(ref, k) for ref, count in zip(block_refs, block_counts) for k in range(count)]
    channels, cap, _ = env_refs[0].shape
    build_mixers(mpo_ref, site, plan, mixer_refs)
    for k, (ref, place) in enumerate(blocks):
        flipped_ref[k] = ref[place].T
    for env_ref, mixer_ref, mixed_ref in zip(env_refs, mixer_refs, mixed_refs):
        count = mixed_ref.shape[0]

        def mix(g, _):
            rows = pl.ds(pl.multiple_of(g * ROWS, ROWS), ROWS)
            piece = env_ref[:, rows, :].reshape(channels * ROWS, cap)
            mixed = jnp.dot(mixer_ref[...], piece, preferred_element_type=jnp.float32)
            mixed_ref[:, rows, :] = mixed.astype(jnp.bfloat16).reshape(count, ROWS, cap)
            return 0

        lax.fori_loop(0, cap // ROWS, mix, 0, unroll=4)
    for part, (low, high) in enumerate(zip(cuts[:-1], cuts[1:])):

        def channel(v, _):
            totals = [None] * outputs
            if based:
                totals = [ref[low + v].astype(jnp.float32) for ref in base_refs]
            for source, states in enumerate(plan):
                for place, (_, block, out) in enumerate(states):
                    ref, k = blocks[block]
                    blended = jnp.dot(
                        mixed_refs[source][place * channels + low + v], ref[k], preferred_element_type=jnp.float32
                    ).astype(jnp.bfloat16)
                    one = jnp.dot(flipped_ref[block], blended, preferred_element_type=jnp.float32)
                    totals[out] = one if totals[out] is None else totals[out] + one
            for out, total in enumerate(totals):
                out_refs[out][part][v] = total.astype(jnp.bfloat16)
            return 0

        lax.fori_loop(0, high - low, channel, 0, unroll=UNROLL)


def products(site, plan, cuts, envs, base, mpo, blocks):
    channels, cap, _ = envs[0].shape
    outputs = 1 + max(out for states in plan for _, _, out in states)
    work = sum(len(states) for states in plan)
    counts = [block.shape[0] for block in blocks]
    span = channels * ROWS
    operands = (*envs, *base, mpo, *blocks)
    results = pl.pallas_call(
        lambda *refs: product_kernel(site, plan, cuts, bool(base), counts, *refs),
        out_shape=[
            jax.ShapeDtypeStruct((high - low, cap, cap), jnp.bfloat16)
            for _ in range(outputs) for low, high in zip(cuts[:-1], cuts[1:])
        ],
        in_specs=[pl.BlockSpec(memory_space=pltpu.VMEM)] * len(operands),
        out_specs=[pl.BlockSpec(memory_space=pltpu.VMEM)] * (outputs * (len(cuts) - 1)),
        scratch_shapes=[pltpu.VMEM((len(states) * channels, cap, cap), jnp.bfloat16) for states in plan]
        + [pltpu.VMEM((len(states) * span, span), jnp.bfloat16) for states in plan]
        + [pltpu.VMEM((sum(counts), cap, cap), jnp.bfloat16)],
        compiler_params=pltpu.CompilerParams(vmem_limit_bytes=VMEM_BYTES),
        cost_estimate=pl.CostEstimate(
            flops=6 * work * channels * cap**3, bytes_accessed=4 * 2**20, transcendentals=0
        ),
    )(*operands)
    parts = len(cuts) - 1
    return [results[k * parts:(k + 1) * parts] for k in range(outputs)]


def masked_blocks(site_block_tensors, block_mask, sector_dims):
    capacity = site_block_tensors.shape[-1]
    sector_total = lax.axis_size("sec")
    sector_id = lax.axis_index("sec")
    offsets = jnp.array([0, ND, 1, ND + 1])
    down_step = jnp.array([0, 0, 1, 1])
    targets = sector_id + offsets
    allowed = (targets < sector_total) & ((down_step == 0) | (sector_id % ND < ND - 1))
    sectors = jnp.arange(sector_total)
    own_dims = jnp.sum(jnp.where(sectors == sector_id, sector_dims, 0))
    target_dims = jnp.sum(
        jnp.where(sectors[None, :] == targets[:, None], sector_dims[None, :], 0), axis=1
    )
    target_dims = jnp.where(allowed, target_dims, 0)
    line = jnp.arange(capacity)
    row_live = line < own_dims
    col_live = line[None, :] < target_dims[:, None]
    present = (block_mask[:, 0] * allowed.astype(jnp.int32)).astype(jnp.bfloat16)
    live = row_live[None, :, None] & col_live[:, None, :]
    return jnp.where(live[None], site_block_tensors[:, 0] * present[:, :, None, None], 0)


def two_rows(boundary_env, site_block_tensors, mpo_tensors, block_mask, sector_dims):
    env = boundary_env[0, 0]
    channels = env.shape[0]
    near_env = shift_column(env)
    up_blocks, column_blocks, first_blocks, last_blocks = mask_blocks(site_block_tensors, block_mask, sector_dims)
    near_blocks = shift_column(up_blocks)
    below = lax.ppermute(column_blocks, "sec", [(ND + j, j) for j in range(ND)])
    whole = (0, channels)
    (own,), (own_below,) = products(
        0, (((0, 0, 0), (1, 1, 1)),), whole, (env,), (), mpo_tensors, (first_blocks,)
    )
    (middle,), (middle_below,) = products(
        0, (((2, 0, 0), (3, 1, 1)),), whole, (near_env,), (own, own_below), mpo_tensors, (near_blocks,)
    )
    cuts = tuple(-(-channels * k // PARTS) for k in range(PARTS + 1))
    up, up_below, stay, stay_below = products(
        1, (((0, 0, 2), (1, 1, 3), (2, 2, 0), (3, 3, 1)), ((0, 4, 3), (2, 5, 1))), cuts,
        (middle, middle_below), (), mpo_tensors, (last_blocks, below),
    )
    handed = []
    for part in range(len(cuts) - 1):
        arrived_below = shift_column(up_below[part])
        arrived = shift_column(up[part])
        total_below = (stay_below[part].astype(jnp.float32) + arrived_below.astype(jnp.float32)).astype(jnp.bfloat16)
        from_up = from_behind(total_below, "sec", ND)
        total = stay[part].astype(jnp.float32) + arrived.astype(jnp.float32)
        total = (total + from_up.astype(jnp.float32)).astype(jnp.bfloat16)
        handed.append(from_behind(total, "seg", 1))
    return jnp.concatenate(handed)[None, None]


def contract(left_environ_tensor, block_list, weight_factors):
    merged_mixture = jnp.einsum(
        "umi,ue->emi", left_environ_tensor, weight_factors, preferred_element_type=jnp.float32
    ).astype(jnp.bfloat16)
    combined_mixture = jnp.einsum(
        "gip,pq->giq", merged_mixture, block_list, preferred_element_type=jnp.float32
    ).astype(jnp.bfloat16)
    return jnp.einsum(
        "ba,vbc->vac", block_list, combined_mixture, preferred_element_type=jnp.float32
    ).astype(jnp.bfloat16)


def any_rows(boundary_env, site_block_tensors, mpo_tensors, block_mask, sector_dims):
    blocks = masked_blocks(site_block_tensors, block_mask, sector_dims)
    env = boundary_env[0, 0]
    for n in range(blocks.shape[0]):
        parts = [contract(env, blocks[n, s], mpo_tensors[n, s]) for s in range(4)]
        total = parts[0].astype(jnp.float32) + from_behind(parts[1], "sec", ND).astype(jnp.float32)
        total = total + from_behind(parts[2], "sec", 1).astype(jnp.float32)
        total = total + from_behind(parts[3], "sec", ND + 1).astype(jnp.float32)
        env = total.astype(jnp.bfloat16)
    return from_behind(env, "seg", 1)[None, None]


def solution(mesh):
    in_specs = (
        P("seg", "sec", None, None, None),
        P("seg", "sec", None, None, None),
        P("seg", None, None, None),
        P("seg", "sec", None),
        P(),
    )
    out_specs = P("seg", "sec", None, None, None)
    body = two_rows if mesh.shape["sec"] == 2 * ND else any_rows
    return jax.shard_map(body, mesh=mesh, in_specs=in_specs, out_specs=out_specs, check_vma=False)
```

```python
import jax
import jax.numpy as jnp
from jax import lax
from jax.experimental import pallas as pl
from jax.experimental.pallas import tpu as pltpu
from jax.sharding import PartitionSpec as P

ND = 4
ROWS = 16
PARTS = 4
LAG = 2
VMEM_BYTES = 56 * 2**20


def from_behind(shard, axis, by):
    count = lax.axis_size(axis)
    pairs = [(i, i + by) for i in range(count) if 0 <= i + by < count]
    return lax.ppermute(shard, axis, pairs)


def shift_column(shard):
    count = lax.axis_size("sec")
    return lax.ppermute(shard, "sec", [(q, q + 1) for q in range(count - 1) if q % ND < ND - 1])


TAKEN = ((0, (2, 3)), (1, (0, 2)), (0, (0, 1)), (1, (0, 1, 2, 3)))


def prepare_kernel(site_ref, mask_ref, dims_ref, mpo_ref, mixer_ref, *out_refs):
    cap = site_ref.shape[-1]
    total = dims_ref.shape[0]
    q = lax.axis_index("sec")
    rows = lax.broadcasted_iota(jnp.int32, (cap, cap), 0)
    columns = lax.broadcasted_iota(jnp.int32, (cap, cap), 1)
    own = rows < dims_ref[q]
    for out_ref, (site, states) in zip(out_refs, TAKEN):
        for place, s in enumerate(states):
            target = q + (0, ND, 1, ND + 1)[s]
            allowed = (mask_ref[site, 0, s] > 0) & (target < total)
            if s >= 2:
                allowed = allowed & (q % ND < ND - 1)
            width = jnp.where(allowed, dims_ref[jnp.minimum(target, total - 1)], 0)
            out_ref[place] = jnp.where(own & (columns < width), site_ref[site, 0, s], 0).astype(jnp.bfloat16)
    sites, states, channels, _ = mpo_ref.shape
    span = channels * ROWS
    spread = (
        lax.broadcasted_iota(jnp.int32, (span, channels), 0) // ROWS
        == lax.broadcasted_iota(jnp.int32, (span, channels), 1)
    ).astype(jnp.bfloat16)
    same_row = (
        lax.broadcasted_iota(jnp.int32, (span, span), 0) % ROWS
        == lax.broadcasted_iota(jnp.int32, (span, span), 1) % ROWS
    )
    contract_last = (((1,), (1,)), ((), ()))
    for site in range(sites):
        for s in range(states):
            tall = lax.dot_general(spread, mpo_ref[site, s], contract_last, preferred_element_type=jnp.float32)
            wide = lax.dot_general(
                tall.astype(jnp.bfloat16), spread, contract_last, preferred_element_type=jnp.float32
            )
            mixer_ref[site, s] = jnp.where(same_row, wide, 0.0).astype(jnp.bfloat16)


def prepare(site_block_tensors, block_mask, sector_dims, mpo_tensors):
    cap = site_block_tensors.shape[-1]
    span = mpo_tensors.shape[-1] * ROWS
    vmem, smem = pl.BlockSpec(memory_space=pltpu.VMEM), pl.BlockSpec(memory_space=pltpu.SMEM)
    return pl.pallas_call(
        prepare_kernel,
        out_shape=[jax.ShapeDtypeStruct((*mpo_tensors.shape[:2], span, span), jnp.bfloat16)]
        + [jax.ShapeDtypeStruct((len(states), cap, cap), jnp.bfloat16) for _, states in TAKEN],
        in_specs=[vmem, smem, smem, vmem],
        out_specs=[vmem] * (1 + len(TAKEN)),
        compiler_params=pltpu.CompilerParams(vmem_limit_bytes=VMEM_BYTES),
        cost_estimate=pl.CostEstimate(flops=10**6, bytes_accessed=2 * 2**20, transcendentals=0),
    )(site_block_tensors, block_mask, sector_dims, mpo_tensors)


def mix(mixer_ref, site, states, env_ref, mixed_ref):
    channels, cap, _ = env_ref.shape
    for g in range(0, cap, ROWS):
        piece = env_ref[:, g:g + ROWS, :].reshape(channels * ROWS, cap)
        for k, state in enumerate(states):
            mixed = jnp.dot(mixer_ref[site, state], piece, preferred_element_type=jnp.float32)
            mixed_ref[k, :, g:g + ROWS, :] = mixed.astype(jnp.bfloat16).reshape(channels, ROWS, cap)


def add_products(terms, v, total=None):
    for mixed_ref, block, flipped in terms:
        blended = jnp.dot(mixed_ref[v], block[...], preferred_element_type=jnp.float32).astype(jnp.bfloat16)
        one = jnp.dot(flipped[...], blended, preferred_element_type=jnp.float32)
        total = one if total is None else total + one
    return total.astype(jnp.bfloat16)


def own_kernel(env_ref, mixer_ref, block_ref, own_ref, below_ref, mixed_ref, flipped_ref):
    for k in range(2):
        flipped_ref[k] = block_ref[k].T
    mix(mixer_ref, 0, (0, 1), env_ref, mixed_ref)
    for k, out_ref in enumerate((own_ref, below_ref)):
        for v in range(env_ref.shape[0]):
            out_ref[v] = add_products([(mixed_ref.at[k], block_ref.at[k], flipped_ref.at[k])], v)


def up_kernel(
    near_ref, own_ref, own_below_ref, mixer_ref, near_block_ref, last_ref, column_ref,
    middle_ref, middle_below_ref, *refs,
):
    up_refs, (mixed_ref, mixed_below_ref, flipped_ref) = refs[:-3], refs[-3:]
    channels = near_ref.shape[0]
    for k, block in enumerate((near_block_ref.at[0], near_block_ref.at[1], last_ref.at[2], last_ref.at[3], column_ref.at[1])):
        flipped_ref[k] = block[...].T
    mix(mixer_ref, 0, (2, 3), near_ref, mixed_ref)
    for k, (out_ref, base_ref) in enumerate(((middle_ref, own_ref), (middle_below_ref, own_below_ref))):
        for v in range(channels):
            term = (mixed_ref.at[k], near_block_ref.at[k], flipped_ref.at[k])
            out_ref[v] = add_products([term], v, base_ref[v].astype(jnp.float32))
    mix(mixer_ref, 1, (2, 3), middle_ref, mixed_ref)
    mix(mixer_ref, 1, (2,), middle_below_ref, mixed_below_ref)
    same = [(mixed_ref.at[0], last_ref.at[2], flipped_ref.at[2])]
    down = [
        (mixed_ref.at[1], last_ref.at[3], flipped_ref.at[3]),
        (mixed_below_ref.at[0], column_ref.at[1], flipped_ref.at[4]),
    ]
    v = 0
    for out_ref in up_refs:
        width = out_ref.shape[0] // 2
        for place in range(width):
            out_ref[place] = add_products(down, v + place)
        for place in range(width):
            out_ref[width + place] = add_products(same, v + place)
        v += width


def stay_kernel(middle_ref, middle_below_ref, mixer_ref, last_ref, column_ref, *refs):
    out_refs, (mixed_ref, mixed_below_ref, flipped_ref) = refs[:-3], refs[-3:]
    for k, block in enumerate((last_ref.at[0], last_ref.at[1], column_ref.at[0])):
        flipped_ref[k] = block[...].T
    mix(mixer_ref, 1, (0, 1), middle_ref, mixed_ref)
    mix(mixer_ref, 1, (0,), middle_below_ref, mixed_below_ref)
    same = [(mixed_ref.at[0], last_ref.at[0], flipped_ref.at[0])]
    down = [
        (mixed_ref.at[1], last_ref.at[1], flipped_ref.at[1]),
        (mixed_below_ref.at[0], column_ref.at[0], flipped_ref.at[2]),
    ]
    v = 0
    for out_ref in out_refs:
        width = out_ref.shape[0] // 2
        for place in range(width):
            out_ref[place] = add_products(down, v + place)
        for place in range(width):
            out_ref[width + place] = add_products(same, v + place)
        v += width


def call(kernel, operands, widths, mixed, flipped, work):
    channels, cap, _ = operands[0].shape
    return pl.pallas_call(
        kernel,
        out_shape=[jax.ShapeDtypeStruct((width, cap, cap), jnp.bfloat16) for width in widths],
        in_specs=[pl.BlockSpec(memory_space=pltpu.VMEM)] * len(operands),
        out_specs=[pl.BlockSpec(memory_space=pltpu.VMEM)] * len(widths),
        scratch_shapes=[pltpu.VMEM((n, channels, cap, cap), jnp.bfloat16) for n in mixed]
        + [pltpu.VMEM((flipped, cap, cap), jnp.bfloat16)],
        compiler_params=pltpu.CompilerParams(vmem_limit_bytes=VMEM_BYTES),
        cost_estimate=pl.CostEstimate(
            flops=6 * work * channels * cap**3, bytes_accessed=4 * 2**20, transcendentals=0
        ),
    )(*operands)


def masked_blocks(site_block_tensors, block_mask, sector_dims):
    capacity = site_block_tensors.shape[-1]
    sector_total = lax.axis_size("sec")
    sector_id = lax.axis_index("sec")
    offsets = jnp.array([0, ND, 1, ND + 1])
    down_step = jnp.array([0, 0, 1, 1])
    targets = sector_id + offsets
    allowed = (targets < sector_total) & ((down_step == 0) | (sector_id % ND < ND - 1))
    sectors = jnp.arange(sector_total)
    own_dims = jnp.sum(jnp.where(sectors == sector_id, sector_dims, 0))
    target_dims = jnp.sum(
        jnp.where(sectors[None, :] == targets[:, None], sector_dims[None, :], 0), axis=1
    )
    target_dims = jnp.where(allowed, target_dims, 0)
    line = jnp.arange(capacity)
    row_live = line < own_dims
    col_live = line[None, :] < target_dims[:, None]
    present = (block_mask[:, 0] * allowed.astype(jnp.int32)).astype(jnp.bfloat16)
    live = row_live[None, :, None] & col_live[:, None, :]
    return jnp.where(live[None], site_block_tensors[:, 0] * present[:, :, None, None], 0)


def after(value, *others):
    return lax.optimization_barrier((value, *others))[0]


def cut(count, parts):
    edges = [-(-count * k // parts) for k in range(parts + 1)]
    return list(zip(edges[:-1], edges[1:]))


def wide_add(*terms):
    total = terms[0].astype(jnp.float32)
    for term in terms[1:]:
        total = total + term.astype(jnp.float32)
    return total.astype(jnp.bfloat16)


def two_rows(boundary_env, site_block_tensors, mpo_tensors, block_mask, sector_dims):
    env = boundary_env[0, 0]
    channels = env.shape[0]
    near_env = shift_column(env)
    mixers, up_blocks, column_blocks, first_blocks, last_blocks = prepare(
        site_block_tensors, block_mask, sector_dims, mpo_tensors
    )
    near_blocks = shift_column(up_blocks)
    column = lax.ppermute(column_blocks, "sec", [(ND + j, j) for j in range(ND)])
    own, own_below = call(own_kernel, (env, mixers, first_blocks), (channels,) * 2, (2,), 2, 2)
    pairs = [2 * (high - low) for low, high in cut(channels, PARTS)]
    middle, middle_below, *up = call(
        up_kernel, (near_env, own, own_below, mixers, near_blocks, last_blocks, column),
        (channels, channels, *pairs), (2, 1), 5, 5,
    )
    arrived = [shift_column(x) for x in up]
    stay = call(stay_kernel, (middle, middle_below, mixers, last_blocks, column), pairs, (2, 1), 3, 3)
    below, handed, last = [], [], None
    for step in range(PARTS + LAG):
        if step < PARTS:
            width = pairs[step] // 2
            there = arrived[step] if last is None else after(arrived[step], last)
            last = wide_add(stay[step][:width], there[:width])
            below.append(from_behind(last, "sec", ND))
        if step >= LAG:
            part = step - LAG
            width = pairs[part] // 2
            last = wide_add(stay[part][width:], arrived[part][width:], after(below[part], last))
            handed.append(from_behind(last, "seg", 1))
    return jnp.concatenate(handed)[None, None]


def contract(left_environ_tensor, block_list, weight_factors):
    merged_mixture = jnp.einsum(
        "umi,ue->emi", left_environ_tensor, weight_factors, preferred_element_type=jnp.float32
    ).astype(jnp.bfloat16)
    combined_mixture = jnp.einsum(
        "gip,pq->giq", merged_mixture, block_list, preferred_element_type=jnp.float32
    ).astype(jnp.bfloat16)
    return jnp.einsum(
        "ba,vbc->vac", block_list, combined_mixture, preferred_element_type=jnp.float32
    ).astype(jnp.bfloat16)


def any_rows(boundary_env, site_block_tensors, mpo_tensors, block_mask, sector_dims):
    blocks = masked_blocks(site_block_tensors, block_mask, sector_dims)
    env = boundary_env[0, 0]
    for n in range(blocks.shape[0]):
        parts = [contract(env, blocks[n, s], mpo_tensors[n, s]) for s in range(4)]
        total = parts[0].astype(jnp.float32) + from_behind(parts[1], "sec", ND).astype(jnp.float32)
        total = total + from_behind(parts[2], "sec", 1).astype(jnp.float32)
        total = total + from_behind(parts[3], "sec", ND + 1).astype(jnp.float32)
        env = total.astype(jnp.bfloat16)
    return from_behind(env, "seg", 1)[None, None]


def solution(mesh):
    in_specs = (
        P("seg", "sec", None, None, None),
        P("seg", "sec", None, None, None),
        P("seg", None, None, None),
        P("seg", "sec", None),
        P(),
    )
    out_specs = P("seg", "sec", None, None, None)
    body = two_rows if mesh.shape["sec"] == 2 * ND else any_rows
    return jax.shard_map(body, mesh=mesh, in_specs=in_specs, out_specs=out_specs, check_vma=False)
```

```python
import jax
import jax.numpy as jnp
from jax import lax
from jax.experimental import pallas as pl
from jax.experimental.pallas import tpu as pltpu
from jax.sharding import PartitionSpec as P

ND = 4
ROWS = 16
PARTS = 4
LAG = 2
VMEM_BYTES = 24 * 2**20


def from_behind(shard, axis, by):
    count = lax.axis_size(axis)
    pairs = [(i, i + by) for i in range(count) if 0 <= i + by < count]
    return lax.ppermute(shard, axis, pairs)


def shift_column(shard):
    count = lax.axis_size("sec")
    return lax.ppermute(shard, "sec", [(q, q + 1) for q in range(count - 1) if q % ND < ND - 1])


TAKEN = ((0, (2, 3)), (1, (0, 2)), (0, (0, 1)), (1, (0, 1, 2, 3)))


def prepare_kernel(site_ref, mask_ref, dims_ref, mpo_ref, mixer_ref, *out_refs):
    cap = site_ref.shape[-1]
    total = dims_ref.shape[0]
    q = lax.axis_index("sec")
    rows = lax.broadcasted_iota(jnp.int32, (cap, cap), 0)
    columns = lax.broadcasted_iota(jnp.int32, (cap, cap), 1)
    own = rows < dims_ref[q]
    for out_ref, (site, states) in zip(out_refs, TAKEN):
        for place, s in enumerate(states):
            target = q + (0, ND, 1, ND + 1)[s]
            allowed = (mask_ref[site, 0, s] > 0) & (target < total)
            if s >= 2:
                allowed = allowed & (q % ND < ND - 1)
            width = jnp.where(allowed, dims_ref[jnp.minimum(target, total - 1)], 0)
            out_ref[place] = jnp.where(own & (columns < width), site_ref[site, 0, s], 0).astype(jnp.bfloat16)
    sites, states, channels, _ = mpo_ref.shape
    span = channels * ROWS
    spread = (
        lax.broadcasted_iota(jnp.int32, (span, channels), 0) // ROWS
        == lax.broadcasted_iota(jnp.int32, (span, channels), 1)
    ).astype(jnp.bfloat16)
    same_row = (
        lax.broadcasted_iota(jnp.int32, (span, span), 0) % ROWS
        == lax.broadcasted_iota(jnp.int32, (span, span), 1) % ROWS
    )
    contract_last = (((1,), (1,)), ((), ()))
    for site in range(sites):
        for s in range(states):
            tall = lax.dot_general(spread, mpo_ref[site, s], contract_last, preferred_element_type=jnp.float32)
            wide = lax.dot_general(
                tall.astype(jnp.bfloat16), spread, contract_last, preferred_element_type=jnp.float32
            )
            mixer_ref[site, s] = jnp.where(same_row, wide, 0.0).astype(jnp.bfloat16)


def prepare(site_block_tensors, block_mask, sector_dims, mpo_tensors):
    cap = site_block_tensors.shape[-1]
    span = mpo_tensors.shape[-1] * ROWS
    vmem, smem = pl.BlockSpec(memory_space=pltpu.VMEM), pl.BlockSpec(memory_space=pltpu.SMEM)
    return pl.pallas_call(
        prepare_kernel,
        out_shape=[jax.ShapeDtypeStruct((*mpo_tensors.shape[:2], span, span), jnp.bfloat16)]
        + [jax.ShapeDtypeStruct((len(states), cap, cap), jnp.bfloat16) for _, states in TAKEN],
        in_specs=[vmem, smem, smem, vmem],
        out_specs=[vmem] * (1 + len(TAKEN)),
        compiler_params=pltpu.CompilerParams(vmem_limit_bytes=VMEM_BYTES),
        cost_estimate=pl.CostEstimate(flops=10**6, bytes_accessed=2 * 2**20, transcendentals=0),
    )(site_block_tensors, block_mask, sector_dims, mpo_tensors)


def mix(mixer_ref, site, states, env_ref, mixed_ref):
    channels, cap, _ = env_ref.shape
    for g in range(0, cap, ROWS):
        piece = env_ref[:, g:g + ROWS, :].reshape(channels * ROWS, cap)
        for k, state in enumerate(states):
            mixed = jnp.dot(mixer_ref[site, state], piece, preferred_element_type=jnp.float32)
            mixed_ref[k, :, g:g + ROWS, :] = mixed.astype(jnp.bfloat16).reshape(channels, ROWS, cap)


def add_products(terms, v, total=None):
    for mixed_ref, block, flipped in terms:
        blended = jnp.dot(mixed_ref[v], block[...], preferred_element_type=jnp.float32).astype(jnp.bfloat16)
        one = jnp.dot(flipped[...], blended, preferred_element_type=jnp.float32)
        total = one if total is None else total + one
    return total.astype(jnp.bfloat16)


def own_kernel(env_ref, mixer_ref, block_ref, own_ref, below_ref, mixed_ref, flipped_ref):
    for k in range(2):
        flipped_ref[k] = block_ref[k].T
    mix(mixer_ref, 0, (0, 1), env_ref, mixed_ref)
    for k, out_ref in enumerate((own_ref, below_ref)):
        for v in range(env_ref.shape[0]):
            out_ref[v] = add_products([(mixed_ref.at[k], block_ref.at[k], flipped_ref.at[k])], v)


def up_kernel(
    near_ref, own_ref, own_below_ref, mixer_ref, near_block_ref, last_ref, column_ref,
    middle_ref, middle_below_ref, *refs,
):
    up_refs, (mixed_ref, mixed_below_ref, flipped_ref) = refs[:-3], refs[-3:]
    channels = near_ref.shape[0]
    for k, block in enumerate((near_block_ref.at[0], near_block_ref.at[1], last_ref.at[2], last_ref.at[3], column_ref.at[1])):
        flipped_ref[k] = block[...].T
    mix(mixer_ref, 0, (2, 3), near_ref, mixed_ref)
    for k, (out_ref, base_ref) in enumerate(((middle_ref, own_ref), (middle_below_ref, own_below_ref))):
        for v in range(channels):
            term = (mixed_ref.at[k], near_block_ref.at[k], flipped_ref.at[k])
            out_ref[v] = add_products([term], v, base_ref[v].astype(jnp.float32))
    mix(mixer_ref, 1, (2, 3), middle_ref, mixed_ref)
    mix(mixer_ref, 1, (2,), middle_below_ref, mixed_below_ref)
    same = [(mixed_ref.at[0], last_ref.at[2], flipped_ref.at[2])]
    down = [
        (mixed_ref.at[1], last_ref.at[3], flipped_ref.at[3]),
        (mixed_below_ref.at[0], column_ref.at[1], flipped_ref.at[4]),
    ]
    v = 0
    for out_ref in up_refs:
        width = out_ref.shape[0] // 2
        for place in range(width):
            out_ref[place] = add_products(down, v + place)
        for place in range(width):
            out_ref[width + place] = add_products(same, v + place)
        v += width


def stay_kernel(middle_ref, middle_below_ref, mixer_ref, last_ref, column_ref, *refs):
    out_refs, (mixed_ref, mixed_below_ref, flipped_ref) = refs[:-3], refs[-3:]
    for k, block in enumerate((last_ref.at[0], last_ref.at[1], column_ref.at[0])):
        flipped_ref[k] = block[...].T
    mix(mixer_ref, 1, (0, 1), middle_ref, mixed_ref)
    mix(mixer_ref, 1, (0,), middle_below_ref, mixed_below_ref)
    same = [(mixed_ref.at[0], last_ref.at[0], flipped_ref.at[0])]
    down = [
        (mixed_ref.at[1], last_ref.at[1], flipped_ref.at[1]),
        (mixed_below_ref.at[0], column_ref.at[0], flipped_ref.at[2]),
    ]
    v = 0
    for out_ref in out_refs:
        width = out_ref.shape[0] // 2
        for place in range(width):
            out_ref[place] = add_products(down, v + place)
        for place in range(width):
            out_ref[width + place] = add_products(same, v + place)
        v += width


def call(kernel, operands, widths, mixed, flipped, work):
    channels, cap, _ = operands[0].shape
    return pl.pallas_call(
        kernel,
        out_shape=[jax.ShapeDtypeStruct((width, cap, cap), jnp.bfloat16) for width in widths],
        in_specs=[pl.BlockSpec(memory_space=pltpu.VMEM)] * len(operands),
        out_specs=[pl.BlockSpec(memory_space=pltpu.VMEM)] * len(widths),
        scratch_shapes=[pltpu.VMEM((n, channels, cap, cap), jnp.bfloat16) for n in mixed]
        + [pltpu.VMEM((flipped, cap, cap), jnp.bfloat16)],
        compiler_params=pltpu.CompilerParams(vmem_limit_bytes=VMEM_BYTES),
        cost_estimate=pl.CostEstimate(
            flops=6 * work * channels * cap**3, bytes_accessed=4 * 2**20, transcendentals=0
        ),
    )(*operands)


def masked_blocks(site_block_tensors, block_mask, sector_dims):
    capacity = site_block_tensors.shape[-1]
    sector_total = lax.axis_size("sec")
    sector_id = lax.axis_index("sec")
    offsets = jnp.array([0, ND, 1, ND + 1])
    down_step = jnp.array([0, 0, 1, 1])
    targets = sector_id + offsets
    allowed = (targets < sector_total) & ((down_step == 0) | (sector_id % ND < ND - 1))
    sectors = jnp.arange(sector_total)
    own_dims = jnp.sum(jnp.where(sectors == sector_id, sector_dims, 0))
    target_dims = jnp.sum(
        jnp.where(sectors[None, :] == targets[:, None], sector_dims[None, :], 0), axis=1
    )
    target_dims = jnp.where(allowed, target_dims, 0)
    line = jnp.arange(capacity)
    row_live = line < own_dims
    col_live = line[None, :] < target_dims[:, None]
    present = (block_mask[:, 0] * allowed.astype(jnp.int32)).astype(jnp.bfloat16)
    live = row_live[None, :, None] & col_live[:, None, :]
    return jnp.where(live[None], site_block_tensors[:, 0] * present[:, :, None, None], 0)


def after(value, *others):
    return lax.optimization_barrier((value, *others))[0]


def cut(count, parts):
    edges = [-(-count * k // parts) for k in range(parts + 1)]
    return list(zip(edges[:-1], edges[1:]))


def wide_add(*terms):
    total = terms[0].astype(jnp.float32)
    for term in terms[1:]:
        total = total + term.astype(jnp.float32)
    return total.astype(jnp.bfloat16)


def two_rows(boundary_env, site_block_tensors, mpo_tensors, block_mask, sector_dims):
    env = boundary_env[0, 0]
    channels = env.shape[0]
    near_env = shift_column(env)
    mixers, up_blocks, column_blocks, first_blocks, last_blocks = prepare(
        site_block_tensors, block_mask, sector_dims, mpo_tensors
    )
    near_blocks = shift_column(up_blocks)
    column = lax.ppermute(column_blocks, "sec", [(ND + j, j) for j in range(ND)])
    own, own_below = call(own_kernel, (env, mixers, first_blocks), (channels,) * 2, (2,), 2, 2)
    pairs = [2 * (high - low) for low, high in cut(channels, PARTS)]
    middle, middle_below, *up = call(
        up_kernel, (near_env, own, own_below, mixers, near_blocks, last_blocks, column),
        (channels, channels, *pairs), (2, 1), 5, 5,
    )
    arrived = [shift_column(x) for x in up]
    stay = call(stay_kernel, (middle, middle_below, mixers, last_blocks, column), pairs, (2, 1), 3, 3)
    below, handed, last = [], [], None
    for step in range(PARTS + LAG):
        if step < PARTS:
            width = pairs[step] // 2
            there = arrived[step] if last is None else after(arrived[step], last)
            last = wide_add(stay[step][:width], there[:width])
            below.append(from_behind(last, "sec", ND))
        if step >= LAG:
            part = step - LAG
            width = pairs[part] // 2
            last = wide_add(stay[part][width:], arrived[part][width:], after(below[part], last))
            handed.append(from_behind(last, "seg", 1))
    return jnp.concatenate(handed)[None, None]


def contract(left_environ_tensor, block_list, weight_factors):
    merged_mixture = jnp.einsum(
        "umi,ue->emi", left_environ_tensor, weight_factors, preferred_element_type=jnp.float32
    ).astype(jnp.bfloat16)
    combined_mixture = jnp.einsum(
        "gip,pq->giq", merged_mixture, block_list, preferred_element_type=jnp.float32
    ).astype(jnp.bfloat16)
    return jnp.einsum(
        "ba,vbc->vac", block_list, combined_mixture, preferred_element_type=jnp.float32
    ).astype(jnp.bfloat16)


def any_rows(boundary_env, site_block_tensors, mpo_tensors, block_mask, sector_dims):
    blocks = masked_blocks(site_block_tensors, block_mask, sector_dims)
    env = boundary_env[0, 0]
    for n in range(blocks.shape[0]):
        parts = [contract(env, blocks[n, s], mpo_tensors[n, s]) for s in range(4)]
        total = parts[0].astype(jnp.float32) + from_behind(parts[1], "sec", ND).astype(jnp.float32)
        total = total + from_behind(parts[2], "sec", 1).astype(jnp.float32)
        total = total + from_behind(parts[3], "sec", ND + 1).astype(jnp.float32)
        env = total.astype(jnp.bfloat16)
    return from_behind(env, "seg", 1)[None, None]


def solution(mesh):
    in_specs = (
        P("seg", "sec", None, None, None),
        P("seg", "sec", None, None, None),
        P("seg", None, None, None),
        P("seg", "sec", None),
        P(),
    )
    out_specs = P("seg", "sec", None, None, None)
    body = two_rows if mesh.shape["sec"] == 2 * ND else any_rows
    return jax.shard_map(body, mesh=mesh, in_specs=in_specs, out_specs=out_specs, check_vma=False)
```

```python
import functools

import jax
import jax.numpy as jnp
from jax import lax
from jax.experimental import pallas as pl
from jax.experimental.pallas import tpu as pltpu
from jax.sharding import PartitionSpec as P

ND = 4
CORES = 2
ROWS = 16
EDGES = (0, 5, 9, 13)
LAG = 1
BACK = 2
LONE_STEP = 0
EARLY_FLOPS = 6
LATE_FLOPS = 60
SMALL_FLOPS = 0
VMEM_BYTES = 28 * 2**20


def from_behind(shard, axis, by):
    count = lax.axis_size(axis)
    pairs = [(i, i + by) for i in range(count) if 0 <= i + by < count]
    return lax.ppermute(shard, axis, pairs)


TAKEN = ((0, (2, 3)), (1, (0, 2)), (0, (0, 1)), (1, (0, 1, 2, 3)))


def prepare_kernel(site_ref, mask_ref, dims_ref, mpo_ref, mixer_ref, *out_refs):
    cap = site_ref.shape[-1]
    total = dims_ref.shape[0]
    q = lax.axis_index("sec")
    rows = lax.broadcasted_iota(jnp.int32, (cap, cap), 0)
    columns = lax.broadcasted_iota(jnp.int32, (cap, cap), 1)
    own = rows < dims_ref[q]
    for out_ref, (site, states) in zip(out_refs, TAKEN):
        for place, s in enumerate(states):
            target = q + (0, ND, 1, ND + 1)[s]
            allowed = (mask_ref[site, 0, s] > 0) & (target < total)
            if s >= 2:
                allowed = allowed & (q % ND < ND - 1)
            width = jnp.where(allowed, dims_ref[jnp.minimum(target, total - 1)], 0)
            out_ref[place] = jnp.where(own & (columns < width), site_ref[site, 0, s], 0).astype(jnp.bfloat16)
    sites, states, channels, _ = mpo_ref.shape
    span = channels * ROWS
    spread = (
        lax.broadcasted_iota(jnp.int32, (span, channels), 0) // ROWS
        == lax.broadcasted_iota(jnp.int32, (span, channels), 1)
    ).astype(jnp.bfloat16)
    same_row = (
        lax.broadcasted_iota(jnp.int32, (span, span), 0) % ROWS
        == lax.broadcasted_iota(jnp.int32, (span, span), 1) % ROWS
    )
    contract_last = (((1,), (1,)), ((), ()))
    for site in range(sites):
        for s in range(states):
            tall = lax.dot_general(spread, mpo_ref[site, s], contract_last, preferred_element_type=jnp.float32)
            wide = lax.dot_general(
                tall.astype(jnp.bfloat16), spread, contract_last, preferred_element_type=jnp.float32
            )
            mixer_ref[site, s] = jnp.where(same_row, wide, 0.0).astype(jnp.bfloat16)


def prepare(site_block_tensors, block_mask, sector_dims, mpo_tensors):
    cap = site_block_tensors.shape[-1]
    span = mpo_tensors.shape[-1] * ROWS
    vmem, smem = pl.BlockSpec(memory_space=pltpu.VMEM), pl.BlockSpec(memory_space=pltpu.SMEM)
    return pl.pallas_call(
        prepare_kernel,
        out_shape=[jax.ShapeDtypeStruct((*mpo_tensors.shape[:2], span, span), jnp.bfloat16)]
        + [jax.ShapeDtypeStruct((len(states), cap, cap), jnp.bfloat16) for _, states in TAKEN],
        in_specs=[vmem, smem, smem, vmem],
        out_specs=[vmem] * (1 + len(TAKEN)),
        compiler_params=pltpu.CompilerParams(vmem_limit_bytes=VMEM_BYTES),
        cost_estimate=pl.CostEstimate(flops=10**6, bytes_accessed=2 * 2**20, transcendentals=0),
    )(site_block_tensors, block_mask, sector_dims, mpo_tensors)


def mix(mixer_ref, site, states, env_ref, mixed_ref):
    channels, cap, _ = env_ref.shape
    for g in range(0, cap, ROWS):
        piece = env_ref[:, g:g + ROWS, :].reshape(channels * ROWS, cap)
        for k, state in enumerate(states):
            mixed = jnp.dot(mixer_ref[site, state], piece, preferred_element_type=jnp.float32)
            mixed_ref[k, :, g:g + ROWS, :] = mixed.astype(jnp.bfloat16).reshape(channels, ROWS, cap)


def add_products(terms, v, total=None):
    for mixed_ref, block, flipped in terms:
        blended = jnp.dot(mixed_ref[v], block[...], preferred_element_type=jnp.float32).astype(jnp.bfloat16)
        one = jnp.dot(flipped[...], blended, preferred_element_type=jnp.float32)
        total = one if total is None else total + one
    return total.astype(jnp.bfloat16)


def own_kernel(env_ref, mixer_ref, block_ref, own_ref, below_ref, mixed_ref, flipped_ref):
    for k in range(2):
        flipped_ref[k] = block_ref[k].T
    mix(mixer_ref, 0, (0, 1), env_ref, mixed_ref)
    for k, out_ref in enumerate((own_ref, below_ref)):
        for v in range(env_ref.shape[0]):
            out_ref[v] = add_products([(mixed_ref.at[k], block_ref.at[k], flipped_ref.at[k])], v)


def is_x_receiver():
    j = lax.axis_index("sec") % ND
    return (j % CORES == 0) & (j > 0)


def up_kernel(
    kept, near_ref, own_ref, own_below_ref, mixer_ref, near_block_ref, last_ref, column_ref, *refs,
):
    remain_ref, *up_refs = refs[kept:-4]
    up_refs = up_refs[max(kept - 1, 0):]
    middle_ref, mixed_ref, mixed_below_ref, flipped_ref = refs[-4:]
    channels = near_ref.shape[0]

    @pl.when(is_x_receiver() if kept else jnp.logical_not(is_x_receiver()))
    def _():
        blocks = (near_block_ref.at[0], near_block_ref.at[1], last_ref.at[2], last_ref.at[3], column_ref.at[1])
        for k, block in enumerate(blocks):
            flipped_ref[k] = block[...].T
        mix(mixer_ref, 0, (2, 3), near_ref, mixed_ref)
        for k, base_ref in enumerate((own_ref, own_below_ref)):
            for v in range(channels):
                term = (mixed_ref.at[k], near_block_ref.at[k], flipped_ref.at[k])
                middle_ref[k, v] = add_products([term], v, base_ref[v].astype(jnp.float32))
        mix(mixer_ref, 1, (2, 3), middle_ref.at[0], mixed_ref)
        mix(mixer_ref, 1, (2,), middle_ref.at[1], mixed_below_ref)
        same = [(mixed_ref.at[0], last_ref.at[2], flipped_ref.at[2])]
        down = [
            (mixed_ref.at[1], last_ref.at[3], flipped_ref.at[3]),
            (mixed_below_ref.at[0], column_ref.at[1], flipped_ref.at[4]),
        ]
        v = 0
        for out_ref in up_refs:
            width = out_ref.shape[0] // 2
            for place in range(width):
                out_ref[place] = add_products(down, v + place)
            for place in range(width):
                out_ref[width + place] = add_products(same, v + place)
            v += width
        mix(mixer_ref, 1, (0, 1), middle_ref.at[0], remain_ref.at[pl.ds(0, 2)])
        mix(mixer_ref, 1, (0,), middle_ref.at[1], remain_ref.at[pl.ds(2, 1)])


def lone_kernel(own_ref, own_below_ref, mixer_ref, last_ref, column_ref, below_ref, same_ref, mixed_ref, flipped_ref):
    @pl.when(lax.axis_index("sec") % ND == 0)
    def _():
        mix(mixer_ref, 1, (0, 1), own_ref, mixed_ref.at[pl.ds(0, 2)])
        mix(mixer_ref, 1, (0,), own_below_ref, mixed_ref.at[pl.ds(2, 1)])
        remain(mixed_ref, last_ref, column_ref, flipped_ref, below_ref, same_ref, 0, ())


def remain_kernel(low, remain_ref, last_ref, column_ref, *refs):
    arrived_refs, (below_ref, same_ref, flipped_ref) = refs[:-3], refs[-3:]

    @pl.when(lax.axis_index("sec") % ND > 0)
    def _():
        arrived = [(ref, 0, below_ref.shape[0]) for ref in arrived_refs]
        remain(remain_ref, last_ref, column_ref, flipped_ref, below_ref, same_ref, low, arrived)


def remain(mixed_ref, last_ref, column_ref, flipped_ref, below_ref, same_ref, low, arrived):
    for k, block in enumerate((last_ref.at[0], last_ref.at[1], column_ref.at[0])):
        flipped_ref[k] = block[...].T
    same = [(mixed_ref.at[0], last_ref.at[0], flipped_ref.at[0])]
    down = [
        (mixed_ref.at[1], last_ref.at[1], flipped_ref.at[1]),
        (mixed_ref.at[2], column_ref.at[0], flipped_ref.at[2]),
    ]
    for row, (terms, out_ref) in enumerate(((down, below_ref), (same, same_ref))):
        for k in range(out_ref.shape[0]):
            total = None
            for arrived_ref, *begins in arrived:
                there = arrived_ref[begins[row] + k].astype(jnp.float32)
                total = there if total is None else total + there
            out_ref[k] = add_products(terms, low + k, total)


def call(kernel, operands, shapes, scratch, work, aliased=(), flops=6):
    cap = operands[0].shape[-1]
    vmem = pl.BlockSpec(memory_space=pltpu.VMEM)
    return pl.pallas_call(
        kernel,
        out_shape=[jax.ShapeDtypeStruct((*shape, cap, cap), jnp.bfloat16) for shape in shapes],
        in_specs=[vmem] * (len(operands) + len(aliased)),
        out_specs=[vmem] * len(shapes),
        input_output_aliases={len(operands) + k: k for k in range(len(aliased))},
        scratch_shapes=[pltpu.VMEM((*shape, cap, cap), jnp.bfloat16) for shape in scratch],
        compiler_params=pltpu.CompilerParams(vmem_limit_bytes=VMEM_BYTES),
        cost_estimate=pl.CostEstimate(flops=flops * work * cap**3, bytes_accessed=flops * 2**19, transcendentals=0),
    )(*operands, *aliased)


def masked_blocks(site_block_tensors, block_mask, sector_dims):
    capacity = site_block_tensors.shape[-1]
    sector_total = lax.axis_size("sec")
    sector_id = lax.axis_index("sec")
    offsets = jnp.array([0, ND, 1, ND + 1])
    down_step = jnp.array([0, 0, 1, 1])
    targets = sector_id + offsets
    allowed = (targets < sector_total) & ((down_step == 0) | (sector_id % ND < ND - 1))
    sectors = jnp.arange(sector_total)
    own_dims = jnp.sum(jnp.where(sectors == sector_id, sector_dims, 0))
    target_dims = jnp.sum(
        jnp.where(sectors[None, :] == targets[:, None], sector_dims[None, :], 0), axis=1
    )
    target_dims = jnp.where(allowed, target_dims, 0)
    line = jnp.arange(capacity)
    row_live = line < own_dims
    col_live = line[None, :] < target_dims[:, None]
    present = (block_mask[:, 0] * allowed.astype(jnp.int32)).astype(jnp.bfloat16)
    live = row_live[None, :, None] & col_live[:, None, :]
    return jnp.where(live[None], site_block_tensors[:, 0] * present[:, :, None, None], 0)


def after(value, *others):
    return lax.optimization_barrier((value, *others))[0]


def cut(count):
    edges = [-(-count * k // EDGES[-1]) for k in EDGES]
    return [high - low for low, high in zip(edges[:-1], edges[1:])]


def wide_add(*terms):
    total = terms[0].astype(jnp.float32)
    for term in terms[1:]:
        total = total + term.astype(jnp.float32)
    return total.astype(jnp.bfloat16)


def two_rows(boundary_env, site_block_tensors, mpo_tensors, block_mask, sector_dims):
    env = boundary_env[0, 0]
    channels = env.shape[0]
    count = lax.axis_size("sec")

    def send(shard, sources, seg, sec):
        pairs = [
            (g * count + q, (g + seg) * count + q + sec)
            for g in range(lax.axis_size("seg") - seg) for q in sources
        ]
        return lax.ppermute(shard, ("seg", "sec"), pairs)

    steps = [(q, q + 1) for q in range(count - 1) if q % ND < ND - 1]
    over_x = [pair for pair in steps if pair[1] % CORES == 0]
    on_chip = [pair for pair in steps if pair[1] % CORES]
    late_on_chip = [pair for pair in on_chip if pair[0] % ND]
    early = [pair for pair in steps if pair not in late_on_chip]
    env_over_x = lax.ppermute(env, "sec", over_x)
    env_on_chip = lax.ppermute(env, "sec", on_chip)
    mixers, up_blocks, column_blocks, first_blocks, last_blocks = prepare(
        site_block_tensors, block_mask, sector_dims, mpo_tensors
    )
    blocks_over_x = lax.ppermute(up_blocks, "sec", over_x)
    blocks_on_chip = lax.ppermute(up_blocks, "sec", on_chip)
    column = lax.ppermute(column_blocks, "sec", [(ND + j, j) for j in range(ND)])
    whole = (channels,)
    own, own_below = call(
        own_kernel, (env, mixers, first_blocks), (whole, whole), ((2, channels), (2,)), 2 * channels
    )
    parts = cut(channels)
    lone_below, lone = call(
        lone_kernel, (own, own_below, mixers, last_blocks, column), (whole, whole), ((3, channels), (3,)),
        3 * channels, (), SMALL_FLOPS,
    )
    lone_from_up = send(lone_below, [0], 0, ND)
    lone_upper = send(lone, [0], 1, 0)
    scratch = ((2, channels), (2, channels), (1, channels), (5,))
    ups = [(2 * width,) for width in parts]
    remaining, *up = call(
        functools.partial(up_kernel, 0),
        (env_on_chip, after(own, lone), own_below, mixers, blocks_on_chip, last_blocks, column),
        ((3, channels), *ups), scratch, 5 * channels, (), EARLY_FLOPS,
    )
    remaining, *late = call(
        functools.partial(up_kernel, len(parts)),
        (env_over_x, own, own_below, mixers, blocks_over_x, last_blocks, column),
        ((3, channels), *ups[1:], *ups), scratch, 5 * channels, (remaining, *up[1:]), LATE_FLOPS,
    )
    arrived = [lax.ppermute(x, "sec", early) for x in (up[0], *late[:len(parts) - 1])]
    late = [lax.ppermute(x, "sec", late_on_chip) for x in late[len(parts) - 1:]]
    rest = [q for q in range(count) if q % ND]
    below, same, handed, last, lone_lower = [], [], [], None, None
    for step in range(len(parts) + LAG):
        if step < len(parts):
            low, width = sum(parts[:step]), parts[step]
            there = after(arrived[step], *((lone_from_up, lone_upper) if last is None else (last,)))
            last, here = call(
                functools.partial(remain_kernel, low), (remaining, last_blocks, column, there, late[step]),
                ((width,), (width,)), ((3,),), 3 * width, (), SMALL_FLOPS,
            )
            same.append(here)
            below.append(send(last, rest[:ND - 1], 0, ND))
        if step == LONE_STEP:
            lone_lower = send(wide_add(lone, after(lone_from_up, last)), [ND], 1, 0)
        if step >= LAG:
            part = step - LAG
            last = wide_add(same[part], after(below[part], last, *handed[:max(part - BACK + 1, 0)]))
            handed.append(send(last, rest, 1, 0))
    return (jnp.concatenate(handed) + (lone_upper + lone_lower))[None, None]


def contract(left_environ_tensor, block_list, weight_factors):
    merged_mixture = jnp.einsum(
        "umi,ue->emi", left_environ_tensor, weight_factors, preferred_element_type=jnp.float32
    ).astype(jnp.bfloat16)
    combined_mixture = jnp.einsum(
        "gip,pq->giq", merged_mixture, block_list, preferred_element_type=jnp.float32
    ).astype(jnp.bfloat16)
    return jnp.einsum(
        "ba,vbc->vac", block_list, combined_mixture, preferred_element_type=jnp.float32
    ).astype(jnp.bfloat16)


def any_rows(boundary_env, site_block_tensors, mpo_tensors, block_mask, sector_dims):
    blocks = masked_blocks(site_block_tensors, block_mask, sector_dims)
    env = boundary_env[0, 0]
    for n in range(blocks.shape[0]):
        parts = [contract(env, blocks[n, s], mpo_tensors[n, s]) for s in range(4)]
        total = parts[0].astype(jnp.float32) + from_behind(parts[1], "sec", ND).astype(jnp.float32)
        total = total + from_behind(parts[2], "sec", 1).astype(jnp.float32)
        total = total + from_behind(parts[3], "sec", ND + 1).astype(jnp.float32)
        env = total.astype(jnp.bfloat16)
    return from_behind(env, "seg", 1)[None, None]


def solution(mesh):
    in_specs = (
        P("seg", "sec", None, None, None),
        P("seg", "sec", None, None, None),
        P("seg", None, None, None),
        P("seg", "sec", None),
        P(),
    )
    out_specs = P("seg", "sec", None, None, None)
    body = two_rows if mesh.shape["sec"] == 2 * ND else any_rows
    return jax.shard_map(body, mesh=mesh, in_specs=in_specs, out_specs=out_specs, check_vma=False)
```

```python
import functools

import jax
import jax.numpy as jnp
from jax import lax
from jax.experimental import pallas as pl
from jax.experimental.pallas import tpu as pltpu
from jax.sharding import PartitionSpec as P

ND = 4
CORES = 2
ROWS = 16
EDGES = (0, 5, 9, 13)
LAG = 1
BACK = 2
LONE_STEP = 0
EARLY_FLOPS = 6
LATE_FLOPS = 60
SMALL_FLOPS = 0
VMEM_BYTES = 28 * 2**20


def from_behind(shard, axis, by):
    count = lax.axis_size(axis)
    pairs = [(i, i + by) for i in range(count) if 0 <= i + by < count]
    return lax.ppermute(shard, axis, pairs)


TAKEN = ((0, (2, 3)), (1, (0, 2)), (0, (0, 1)), (1, (0, 1, 2, 3)))


def prepare_kernel(site_ref, mask_ref, dims_ref, mpo_ref, mixer_ref, *out_refs):
    cap = site_ref.shape[-1]
    total = dims_ref.shape[0]
    q = lax.axis_index("sec")
    rows = lax.broadcasted_iota(jnp.int32, (cap, cap), 0)
    columns = lax.broadcasted_iota(jnp.int32, (cap, cap), 1)
    own = rows < dims_ref[q]
    for out_ref, (site, states) in zip(out_refs, TAKEN):
        for place, s in enumerate(states):
            target = q + (0, ND, 1, ND + 1)[s]
            allowed = (mask_ref[site, 0, s] > 0) & (target < total)
            if s >= 2:
                allowed = allowed & (q % ND < ND - 1)
            width = jnp.where(allowed, dims_ref[jnp.minimum(target, total - 1)], 0)
            out_ref[place] = jnp.where(own & (columns < width), site_ref[site, 0, s], 0).astype(jnp.bfloat16)
    sites, states, channels, _ = mpo_ref.shape
    span = channels * ROWS
    spread = (
        lax.broadcasted_iota(jnp.int32, (span, channels), 0) // ROWS
        == lax.broadcasted_iota(jnp.int32, (span, channels), 1)
    ).astype(jnp.bfloat16)
    same_row = (
        lax.broadcasted_iota(jnp.int32, (span, span), 0) % ROWS
        == lax.broadcasted_iota(jnp.int32, (span, span), 1) % ROWS
    )
    contract_last = (((1,), (1,)), ((), ()))
    for site in range(sites):
        for s in range(states):
            tall = lax.dot_general(spread, mpo_ref[site, s], contract_last, preferred_element_type=jnp.float32)
            wide = lax.dot_general(
                tall.astype(jnp.bfloat16), spread, contract_last, preferred_element_type=jnp.float32
            )
            mixer_ref[site, s] = jnp.where(same_row, wide, 0.0).astype(jnp.bfloat16)


def prepare(site_block_tensors, block_mask, sector_dims, mpo_tensors):
    cap = site_block_tensors.shape[-1]
    span = mpo_tensors.shape[-1] * ROWS
    vmem, smem = pl.BlockSpec(memory_space=pltpu.VMEM), pl.BlockSpec(memory_space=pltpu.SMEM)
    return pl.pallas_call(
        prepare_kernel,
        out_shape=[jax.ShapeDtypeStruct((*mpo_tensors.shape[:2], span, span), jnp.bfloat16)]
        + [jax.ShapeDtypeStruct((len(states), cap, cap), jnp.bfloat16) for _, states in TAKEN],
        in_specs=[vmem, smem, smem, vmem],
        out_specs=[vmem] * (1 + len(TAKEN)),
        compiler_params=pltpu.CompilerParams(vmem_limit_bytes=VMEM_BYTES),
        cost_estimate=pl.CostEstimate(flops=10**6, bytes_accessed=2 * 2**20, transcendentals=0),
    )(site_block_tensors, block_mask, sector_dims, mpo_tensors)


def mix(mixer_ref, site, states, env_ref, mixed_ref):
    channels, cap, _ = env_ref.shape
    for g in range(0, cap, ROWS):
        piece = env_ref[:, g:g + ROWS, :].reshape(channels * ROWS, cap)
        for k, state in enumerate(states):
            mixed = jnp.dot(mixer_ref[site, state], piece, preferred_element_type=jnp.float32)
            mixed_ref[k, :, g:g + ROWS, :] = mixed.astype(jnp.bfloat16).reshape(channels, ROWS, cap)


def add_products(terms, v, total=None):
    for mixed_ref, block, flipped in terms:
        blended = jnp.dot(mixed_ref[v], block[...], preferred_element_type=jnp.float32).astype(jnp.bfloat16)
        one = jnp.dot(flipped[...], blended, preferred_element_type=jnp.float32)
        total = one if total is None else total + one
    return total.astype(jnp.bfloat16)


def own_kernel(env_ref, mixer_ref, block_ref, own_ref, below_ref, mixed_ref, flipped_ref):
    for k in range(2):
        flipped_ref[k] = block_ref[k].T
    mix(mixer_ref, 0, (0, 1), env_ref, mixed_ref)
    for k, out_ref in enumerate((own_ref, below_ref)):
        for v in range(env_ref.shape[0]):
            out_ref[v] = add_products([(mixed_ref.at[k], block_ref.at[k], flipped_ref.at[k])], v)


def is_x_receiver():
    j = lax.axis_index("sec") % ND
    return (j % CORES == 0) & (j > 0)


def up_kernel(
    kept, near_ref, own_ref, own_below_ref, mixer_ref, near_block_ref, last_ref, column_ref, *refs,
):
    remain_ref, *up_refs = refs[kept:-4]
    up_refs = up_refs[max(kept - 1, 0):]
    middle_ref, mixed_ref, mixed_below_ref, flipped_ref = refs[-4:]
    channels = near_ref.shape[0]

    @pl.when(is_x_receiver() if kept else jnp.logical_not(is_x_receiver()))
    def _():
        blocks = (near_block_ref.at[0], near_block_ref.at[1], last_ref.at[2], last_ref.at[3], column_ref.at[1])
        for k, block in enumerate(blocks):
            flipped_ref[k] = block[...].T
        mix(mixer_ref, 0, (2, 3), near_ref, mixed_ref)
        for k, base_ref in enumerate((own_ref, own_below_ref)):
            for v in range(channels):
                term = (mixed_ref.at[k], near_block_ref.at[k], flipped_ref.at[k])
                middle_ref[k, v] = add_products([term], v, base_ref[v].astype(jnp.float32))
        mix(mixer_ref, 1, (2, 3), middle_ref.at[0], mixed_ref)
        mix(mixer_ref, 1, (2,), middle_ref.at[1], mixed_below_ref)
        same = [(mixed_ref.at[0], last_ref.at[2], flipped_ref.at[2])]
        down = [
            (mixed_ref.at[1], last_ref.at[3], flipped_ref.at[3]),
            (mixed_below_ref.at[0], column_ref.at[1], flipped_ref.at[4]),
        ]
        v = 0
        for out_ref in up_refs:
            width = out_ref.shape[0] // 2
            for place in range(width):
                out_ref[place] = add_products(down, v + place)
            for place in range(width):
                out_ref[width + place] = add_products(same, v + place)
            v += width
        mix(mixer_ref, 1, (0, 1), middle_ref.at[0], remain_ref.at[pl.ds(0, 2)])
        mix(mixer_ref, 1, (0,), middle_ref.at[1], remain_ref.at[pl.ds(2, 1)])


def lone_kernel(own_ref, own_below_ref, mixer_ref, last_ref, column_ref, below_ref, same_ref, mixed_ref, flipped_ref):
    @pl.when(lax.axis_index("sec") % ND == 0)
    def _():
        mix(mixer_ref, 1, (0, 1), own_ref, mixed_ref.at[pl.ds(0, 2)])
        mix(mixer_ref, 1, (0,), own_below_ref, mixed_ref.at[pl.ds(2, 1)])
        remain(mixed_ref, last_ref, column_ref, flipped_ref, below_ref, same_ref, 0, ())


def remain_kernel(low, remain_ref, last_ref, column_ref, *refs):
    arrived_refs, (below_ref, same_ref, flipped_ref) = refs[:-3], refs[-3:]

    @pl.when(lax.axis_index("sec") % ND > 0)
    def _():
        arrived = [(ref, 0, below_ref.shape[0]) for ref in arrived_refs]
        remain(remain_ref, last_ref, column_ref, flipped_ref, below_ref, same_ref, low, arrived)


def remain(mixed_ref, last_ref, column_ref, flipped_ref, below_ref, same_ref, low, arrived):
    for k, block in enumerate((last_ref.at[0], last_ref.at[1], column_ref.at[0])):
        flipped_ref[k] = block[...].T
    same = [(mixed_ref.at[0], last_ref.at[0], flipped_ref.at[0])]
    down = [
        (mixed_ref.at[1], last_ref.at[1], flipped_ref.at[1]),
        (mixed_ref.at[2], column_ref.at[0], flipped_ref.at[2]),
    ]
    for row, (terms, out_ref) in enumerate(((down, below_ref), (same, same_ref))):
        for k in range(out_ref.shape[0]):
            total = None
            for arrived_ref, *begins in arrived:
                there = arrived_ref[begins[row] + k].astype(jnp.float32)
                total = there if total is None else total + there
            out_ref[k] = add_products(terms, low + k, total)


def call(kernel, operands, shapes, scratch, work, aliased=(), flops=6):
    cap = operands[0].shape[-1]
    vmem = pl.BlockSpec(memory_space=pltpu.VMEM)
    return pl.pallas_call(
        kernel,
        out_shape=[jax.ShapeDtypeStruct((*shape, cap, cap), jnp.bfloat16) for shape in shapes],
        in_specs=[vmem] * (len(operands) + len(aliased)),
        out_specs=[vmem] * len(shapes),
        input_output_aliases={len(operands) + k: k for k in range(len(aliased))},
        scratch_shapes=[pltpu.VMEM((*shape, cap, cap), jnp.bfloat16) for shape in scratch],
        compiler_params=pltpu.CompilerParams(vmem_limit_bytes=VMEM_BYTES),
        cost_estimate=pl.CostEstimate(flops=flops * work * cap**3, bytes_accessed=flops * 2**19, transcendentals=0),
    )(*operands, *aliased)


def masked_blocks(site_block_tensors, block_mask, sector_dims):
    capacity = site_block_tensors.shape[-1]
    sector_total = lax.axis_size("sec")
    sector_id = lax.axis_index("sec")
    offsets = jnp.array([0, ND, 1, ND + 1])
    down_step = jnp.array([0, 0, 1, 1])
    targets = sector_id + offsets
    allowed = (targets < sector_total) & ((down_step == 0) | (sector_id % ND < ND - 1))
    sectors = jnp.arange(sector_total)
    own_dims = jnp.sum(jnp.where(sectors == sector_id, sector_dims, 0))
    target_dims = jnp.sum(
        jnp.where(sectors[None, :] == targets[:, None], sector_dims[None, :], 0), axis=1
    )
    target_dims = jnp.where(allowed, target_dims, 0)
    line = jnp.arange(capacity)
    row_live = line < own_dims
    col_live = line[None, :] < target_dims[:, None]
    present = (block_mask[:, 0] * allowed.astype(jnp.int32)).astype(jnp.bfloat16)
    live = row_live[None, :, None] & col_live[:, None, :]
    return jnp.where(live[None], site_block_tensors[:, 0] * present[:, :, None, None], 0)


def after(value, *others):
    return lax.optimization_barrier((value, *others))[0]


def cut(count):
    edges = [-(-count * k // EDGES[-1]) for k in EDGES]
    return [high - low for low, high in zip(edges[:-1], edges[1:])]


def wide_add(*terms):
    total = terms[0].astype(jnp.float32)
    for term in terms[1:]:
        total = total + term.astype(jnp.float32)
    return total.astype(jnp.bfloat16)


def two_rows(boundary_env, site_block_tensors, mpo_tensors, block_mask, sector_dims):
    env = boundary_env[0, 0]
    channels = env.shape[0]
    count = lax.axis_size("sec")

    def send(shard, sources, seg, sec):
        pairs = [
            (g * count + q, (g + seg) * count + q + sec)
            for g in range(lax.axis_size("seg") - seg) for q in sources
        ]
        return lax.ppermute(shard, ("seg", "sec"), pairs)

    steps = [(q, q + 1) for q in range(count - 1) if q % ND < ND - 1]
    over_x = [pair for pair in steps if pair[1] % CORES == 0]
    on_chip = [pair for pair in steps if pair[1] % CORES]
    late_on_chip = [pair for pair in on_chip if pair[0] % ND]
    early = [pair for pair in steps if pair not in late_on_chip]
    env_over_x = lax.ppermute(env, "sec", over_x)
    env_on_chip = lax.ppermute(env, "sec", on_chip)
    mixers, up_blocks, column_blocks, first_blocks, last_blocks = prepare(
        site_block_tensors, block_mask, sector_dims, mpo_tensors
    )
    blocks_over_x = lax.ppermute(up_blocks, "sec", over_x)
    blocks_on_chip = lax.ppermute(up_blocks, "sec", on_chip)
    column = lax.ppermute(column_blocks, "sec", [(ND + j, j) for j in range(ND)])
    whole = (channels,)
    own, own_below = call(
        own_kernel, (env, mixers, first_blocks), (whole, whole), ((2, channels), (2,)), 2 * channels
    )
    parts = cut(channels)
    lone_below, lone = call(
        lone_kernel, (own, own_below, mixers, last_blocks, column), (whole, whole), ((3, channels), (3,)),
        3 * channels, (), SMALL_FLOPS,
    )
    lone_from_up = send(lone_below, [0], 0, ND)
    lone_upper = send(lone, [0], 1, 0)
    scratch = ((2, channels), (2, channels), (1, channels), (5,))
    ups = [(2 * width,) for width in parts]
    remaining, *up = call(
        functools.partial(up_kernel, 0),
        (env_on_chip, own, own_below, mixers, blocks_on_chip, last_blocks, column),
        ((3, channels), *ups), scratch, 5 * channels, (), EARLY_FLOPS,
    )
    remaining, *late = call(
        functools.partial(up_kernel, len(parts)),
        (after(env_over_x, lone), own, own_below, mixers, blocks_over_x, last_blocks, column),
        ((3, channels), *ups[1:], *ups), scratch, 5 * channels, (remaining, *up[1:]), LATE_FLOPS,
    )
    arrived = [lax.ppermute(x, "sec", early) for x in (up[0], *late[:len(parts) - 1])]
    late = [lax.ppermute(x, "sec", late_on_chip) for x in late[len(parts) - 1:]]
    rest = [q for q in range(count) if q % ND]
    below, same, handed, last, lone_lower = [], [], [], None, None
    for step in range(len(parts) + LAG):
        if step < len(parts):
            low, width = sum(parts[:step]), parts[step]
            there = after(arrived[step], *((lone_from_up, lone_upper) if last is None else (last,)))
            last, here = call(
                functools.partial(remain_kernel, low), (remaining, last_blocks, column, there, late[step]),
                ((width,), (width,)), ((3,),), 3 * width, (), SMALL_FLOPS,
            )
            same.append(here)
            below.append(send(last, rest[:ND - 1], 0, ND))
        if step == LONE_STEP:
            lone_lower = send(wide_add(lone, after(lone_from_up, last)), [ND], 1, 0)
        if step >= LAG:
            part = step - LAG
            last = wide_add(same[part], after(below[part], last, *handed[:max(part - BACK + 1, 0)]))
            handed.append(send(last, rest, 1, 0))
    return (jnp.concatenate(handed) + (lone_upper + lone_lower))[None, None]


def contract(left_environ_tensor, block_list, weight_factors):
    merged_mixture = jnp.einsum(
        "umi,ue->emi", left_environ_tensor, weight_factors, preferred_element_type=jnp.float32
    ).astype(jnp.bfloat16)
    combined_mixture = jnp.einsum(
        "gip,pq->giq", merged_mixture, block_list, preferred_element_type=jnp.float32
    ).astype(jnp.bfloat16)
    return jnp.einsum(
        "ba,vbc->vac", block_list, combined_mixture, preferred_element_type=jnp.float32
    ).astype(jnp.bfloat16)


def any_rows(boundary_env, site_block_tensors, mpo_tensors, block_mask, sector_dims):
    blocks = masked_blocks(site_block_tensors, block_mask, sector_dims)
    env = boundary_env[0, 0]
    for n in range(blocks.shape[0]):
        parts = [contract(env, blocks[n, s], mpo_tensors[n, s]) for s in range(4)]
        total = parts[0].astype(jnp.float32) + from_behind(parts[1], "sec", ND).astype(jnp.float32)
        total = total + from_behind(parts[2], "sec", 1).astype(jnp.float32)
        total = total + from_behind(parts[3], "sec", ND + 1).astype(jnp.float32)
        env = total.astype(jnp.bfloat16)
    return from_behind(env, "seg", 1)[None, None]


def solution(mesh):
    in_specs = (
        P("seg", "sec", None, None, None),
        P("seg", "sec", None, None, None),
        P("seg", None, None, None),
        P("seg", "sec", None),
        P(),
    )
    out_specs = P("seg", "sec", None, None, None)
    body = two_rows if mesh.shape["sec"] == 2 * ND else any_rows
    return jax.shard_map(body, mesh=mesh, in_specs=in_specs, out_specs=out_specs, check_vma=False)
```
